512 devices in a mesh: pb: 16 (over y, x_hi, core), ma: 32 (over z, x_lo).
Axes of the slice: x: 4 (x_hi: 2, x_lo: 2; x = x_hi * 2 + x_lo), y: 4, z: 16, core: 2. Of those that a mesh axis runs over, the one named last changes fastest.
Arguments:
- queries: bfloat16 [1, 4096, 2048], P(None, ('pb', 'ma')), may hold values from -6 to 6
- map_descriptors: bfloat16 [32768, 2048], P('ma', 'pb'), may hold values from -0.125 to 0.125
- slopes: int32 [8], replicated, may hold values from 0 to 15, as said below
Outputs:
- best: float32 [1, 4096, 32768], P(None, 'pb', 'ma')
The draws below stay inside these ranges and needn't reach their ends.
Inputs may be any that keep to these rules, and one draw needn't show every extreme that they name: `slopes`: 8 distinct velocities; the largest is exactly 15.
All inputs are finite; a program needn't handle non-finite values.
Results may differ from the reference program's by a relative error of at most 0.0003.
Values may be sent and summed in bfloat16 or wider, within the bound.
No kernel may reach another device: no remote copies, remote signals or barrier semaphores. Data moves between devices by JAX's collectives and lax.ppermute only.
A program may use at most 64 MiB of HBM per device.

```python
import math
import jax
import jax.numpy as jnp
from jax import lax

D = 2048
SESS = 1
SEQ = 20
RAD = 10
VMAX = 15
NSLOPE = 8
SPAN = 285
NQ = 4096
NM = 32768


def draw_slopes(key, part):
    order = jax.random.permutation(key, VMAX + 1)[:NSLOPE]
    largest = jnp.max(order)
    return jnp.where(order == largest, VMAX, order).astype(jnp.int32)


def steps_of(key, dims, cuts, smallest, high):
    factor_of = 1.0
    for axis_at, shards_of in cuts:
        heights = jax.random.uniform(jax.random.fold_in(jax.random.fold_in(key, 6), axis_at), (shards_of,), jnp.float32, smallest / len(cuts), high / len(cuts))
        factor_of = factor_of * jnp.repeat(jnp.exp(heights), dims[axis_at] // shards_of).reshape((-1,) + (1,) * (len(dims) - 1 - axis_at))
    return factor_of


def gaussian(key, dims, deviation, bound, cuts=(), held_as=jnp.bfloat16):
    result = jax.random.normal(key, dims, jnp.float32) * deviation
    if len(cuts) > 0:
        result = steps_of(key, dims, cuts, -0.22, 0.18) * result
    return jnp.clip(result, min=-bound, max=bound).astype(held_as)


def setup_inputs(seed: int = 0) -> dict:
    streams_of = jax.random.split(jax.random.key(seed), 4)
    return {
        "queries": gaussian(streams_of[0], (SESS, NQ, D), 1.0, 6.0, ((1, 512),)),
        "map_descriptors": gaussian(streams_of[1], (NM, D), D ** -0.5, 0.125, ((0, 32), (1, 16))),
        "slopes": draw_slopes(jax.random.fold_in(streams_of[3], 71), 0),
    }


def reference(queries, map_descriptors, slopes):

    def one_traversal(query_rows):
        scores = lax.dot_general(query_rows, map_descriptors, (((1,), (1,)), ((), ())), preferred_element_type=jnp.float32)
        padded = jnp.pad(scores, ((0, 0), (RAD, RAD)))
        running = jnp.zeros(scores.shape, jnp.float32)
        squares = jnp.zeros(scores.shape, jnp.float32)
        for offset in range(2 * RAD + 1):
            window = padded[:, offset:offset + NM]
            running = running + window
            squares = squares + window * window
        average = running / (2 * RAD + 1)
        spread = squares / (2 * RAD + 1) - average * average
        normal = (scores - average) / jnp.sqrt(spread + 1.0)
        normal_pad = jnp.pad(normal, ((SEQ - 1, 0), (SPAN, 0)))

        def per_slope(best_val, velocity):
            summed = jnp.zeros((NQ, NM), jnp.float32)
            for lag_step in range(SEQ):
                row_at = jnp.asarray(SEQ - 1 - lag_step, jnp.int32)
                col_at = (SPAN - lag_step * velocity).astype(jnp.int32)
                summed = summed + lax.dynamic_slice(normal_pad, (row_at, col_at), (NQ, NM))
            return (jnp.maximum(best_val, summed), None)
        start_best = jnp.full((NQ, NM), -jnp.inf, jnp.float32)
        best_val, unused = lax.scan(per_slope, start_best, slopes)
        return best_val / math.sqrt(SEQ)
    return lax.map(one_traversal, queries)
```

```python
import functools
import math

import jax
import jax.numpy as jnp
from jax import lax
from jax.experimental import pallas as pl
from jax.experimental.pallas import tpu as pltpu
from jax.sharding import PartitionSpec as P

SEQ = 20
RAD = 10
TOP = 32
LEFT = 384
RIGHT = 128
LANES = 128
CHIPS = 8

FAR = (4, 12, 8)
NEAR = (1, 15, 2)


def along_z(step, cross=0):
    return [
        (z * 2 + side, ((z + step) % 16) * 2 + (side ^ cross))
        for z in range(16)
        for side in range(2)
    ]


def gather_queries(queries):
    depth = queries.shape[-1]
    far = jnp.concatenate(
        [queries[None]] + [lax.ppermute(queries[None], "ma", along_z(k)) for k in FAR]
    )
    other = lax.ppermute(far, "ma", along_z(0, 1))
    side = lax.axis_index("ma") % 2
    first = jnp.where(side == 0, far, other)
    second = jnp.where(side == 0, other, far)
    pairs = jnp.concatenate([first, second], axis=1)
    parts = [pairs] + [lax.ppermute(pairs, "ma", along_z(k)) for k in NEAR]
    held = jnp.stack(parts)
    here = lax.axis_index("ma") // 2
    tail = []
    for z in (14, 15):
        near, far_at = place(z, here)
        tail.append(lax.dynamic_slice(held, (near, far_at, 0, 0), (1, 1, 16, depth)))
    tail = jnp.concatenate(tail).reshape(TOP, depth)
    above = lax.ppermute(tail, "pb", [(i, i + 1) for i in range(15)])
    return held, above


def place(z, here):
    delta = (z - here + 16) % 16
    low = delta % 4
    near = jnp.where(low == 0, 0, jnp.where(low == 3, 1, jnp.where(low == 1, 2, 3)))
    back = jnp.where(low == 0, 0, jnp.where(low == 3, -1, jnp.where(low == 1, 1, -2)))
    rest = ((delta - back + 16) % 16) // 4
    far = jnp.where(rest == 0, 0, jnp.where(rest == 3, 1, jnp.where(rest == 1, 2, 3)))
    return near.astype(jnp.int32), far.astype(jnp.int32)


def gather_map(frames):
    groups = [[2 * i + c for i in range(CHIPS)] for c in range(2)]
    copies = jnp.broadcast_to(frames[None], (CHIPS,) + frames.shape)
    own = lax.all_to_all(copies, "pb", 0, 0, axis_index_groups=groups)
    other = lax.ppermute(own, "pb", [(i, i ^ 1) for i in range(16)])
    return own, other


def score_kernel(at_ref, held_ref, above_ref, own_ref, other_ref, out_ref, left_ref, right_ref, rows_ref):
    rows_ref[:TOP] = above_ref[...]
    for z in range(16):
        rows_ref[TOP + 16 * z : TOP + 16 * z + 16] = held_ref[at_ref[2 * z], at_ref[2 * z + 1]]
    core = at_ref[32]
    columns = own_ref.shape[1]
    width = 256

    def block(n, carry):
        begin = pl.multiple_of(n * width, width)
        total = None
        for g in range(CHIPS):
            one = pl.multiple_of((2 * g + core) * LANES, LANES)
            two = pl.multiple_of((2 * g + 1 - core) * LANES, LANES)
            lhs = jnp.concatenate([rows_ref[:, pl.ds(one, LANES)], rows_ref[:, pl.ds(two, LANES)]], axis=1)
            rhs = jnp.concatenate([own_ref[g, pl.ds(begin, width)], other_ref[g, pl.ds(begin, width)]], axis=1)
            part = lax.dot_general(lhs, rhs, (((1,), (1,)), ((), ())), preferred_element_type=jnp.float32)
            total = part if total is None else total + part
        out_ref[:, pl.ds(begin, width)] = total
        return carry

    lax.fori_loop(0, columns // width, block, 0)
    left_ref[...] = out_ref[:, columns - LEFT :]
    right_ref[...] = out_ref[:, :RIGHT]


def score_tile(at, held, above, own, other):
    rows = TOP + 256
    columns = own.shape[1]
    return pl.pallas_call(
        score_kernel,
        name="scores",
        out_shape=(
            jax.ShapeDtypeStruct((rows, columns), jnp.float32),
            jax.ShapeDtypeStruct((rows, LEFT), jnp.float32),
            jax.ShapeDtypeStruct((rows, RIGHT), jnp.float32),
        ),
        in_specs=[pl.BlockSpec(memory_space=pltpu.SMEM)] + [pl.BlockSpec(memory_space=pltpu.VMEM)] * 4,
        out_specs=(pl.BlockSpec(memory_space=pltpu.VMEM),) * 3,
        scratch_shapes=[pltpu.VMEM((rows, 2048), jnp.bfloat16)],
        compiler_params=pltpu.CompilerParams(vmem_limit_bytes=32 << 20),
        cost_estimate=pl.CostEstimate(flops=2 * rows * columns * 2048, bytes_accessed=8 << 20, transcendentals=0),
    )(at, held, above, own, other)


def tile(c):
    return slice(c * LANES, (c + 1) * LANES)


def best_kernel(slopes_ref, left_ref, mid_ref, right_ref, out_ref, x_ref, two_ref, four_ref, eight_ref):
    rows = mid_ref.shape[0]
    columns = mid_ref.shape[1]
    halo = LEFT // LANES
    tiles = halo + columns // LANES
    first_map = slopes_ref[8] == 0
    step_rows = 96

    def source(c):
        if c < halo:
            return left_ref, c
        if c < tiles:
            return mid_ref, c - halo
        return right_ref, c - tiles

    def up(prev, cur, by, lane):
        return jnp.where(lane < LANES - by, pltpu.roll(prev, LANES - by, 1), pltpu.roll(cur, LANES - by, 1))

    def normalise(block, carry):
        begin = pl.multiple_of(block * 32, 32)
        take = pl.ds(begin, 32)
        lane = lax.broadcasted_iota(jnp.int32, (32, LANES), 1)

        def raw(c):
            ref, at = source(c)
            return ref[take, tile(at)]

        def chain(values):
            one = values
            two = [v + up(v, w, 1, lane) for v, w in zip(one, one[1:] + one[-1:])]
            four = [v + up(v, w, 2, lane) for v, w in zip(two, two[1:] + two[-1:])]
            eight = [v + up(v, w, 4, lane) for v, w in zip(four, four[1:] + four[-1:])]
            ten = [e + up(v, w, 8, lane) for e, v, w in zip(eight, two, two[1:] + two[-1:])]
            twenty = [v + up(v, w, 10, lane) for v, w in zip(ten, ten[1:] + ten[-1:])]
            return [t + up(v, w, 20, lane) for t, v, w in zip(twenty, one, one[1:] + one[-1:])]

        for c in range(tiles):
            near = [raw(max(c - 1, 0)), raw(c), raw(c + 1)]
            sums = chain(near)
            squares = chain([v * v for v in near])
            back = lambda v: jnp.where(lane < RAD, pltpu.roll(v[0], RAD, 1), pltpu.roll(v[1], RAD, 1))
            mean = back(sums) * (1.0 / (2 * RAD + 1))
            square = back(squares) * (1.0 / (2 * RAD + 1))
            value = (near[1] - mean) * lax.rsqrt(square - mean * mean + 1.0)
            if c < halo:
                value = jnp.where(first_map, 0.0, value)
            x_ref[take, tile(c)] = value
        return carry

    lax.fori_loop(0, rows // 32, normalise, 0)

    def shifted(ref, take, c, by, whole, lane, prev):
        at = c if whole is None else pl.multiple_of((c - whole) * LANES, LANES)
        cols = tile(c) if whole is None else pl.ds(at, LANES)
        cur = pltpu.roll(ref[take, cols], by, 1)
        return cur if prev is None else jnp.where(lane < by, prev, cur), cur

    def blocks(start):
        at = start
        while at < rows:
            size = min(64, rows - at)
            yield at, size
            at += size

    def stage(src, dst, lag, by, row0, col0):
        for at, size in blocks(row0):
            lane = lax.broadcasted_iota(jnp.int32, (size, LANES), 1)
            prev = None
            if col0 > 0:
                _, prev = shifted(src, slice(at - lag, at - lag + size), col0 - 1, by, None, lane, None)
            for c in range(col0, tiles):
                moved, prev = shifted(src, slice(at - lag, at - lag + size), c, by, None, lane, prev)
                dst[at : at + size, tile(c)] = src[at : at + size, tile(c)] + moved

    def per_slope(index, carry):
        v = slopes_ref[index]
        stage(x_ref, two_ref, 1, v, 8, 0)
        stage(two_ref, four_ref, 2, 2 * v, 16, 1)
        stage(four_ref, eight_ref, 4, 4 * v, 24, 2)
        by8 = 8 * v
        by16 = 16 * v
        whole = by16 // LANES
        by16 = by16 % LANES
        for at, size in blocks(TOP):
            lane = lax.broadcasted_iota(jnp.int32, (size, LANES), 1)
            take8 = slice(at - 8, at - 8 + size)
            take16 = slice(at - 16, at - 16 + size)
            _, prev8 = shifted(eight_ref, take8, halo - 1, by8, None, lane, None)
            _, prev16 = shifted(four_ref, take16, halo - 1, by16, whole, lane, None)
            for c in range(halo, tiles):
                moved8, prev8 = shifted(eight_ref, take8, c, by8, None, lane, prev8)
                moved16, prev16 = shifted(four_ref, take16, c, by16, whole, lane, prev16)
                total = (eight_ref[at : at + size, tile(c)] + moved8) + moved16
                out_rows = slice(at - TOP, at - TOP + size)
                kept = jnp.where(index == 0, total, jnp.maximum(out_ref[out_rows, tile(c - halo)], total))
                out_ref[out_rows, tile(c - halo)] = kept
        return carry

    lax.fori_loop(0, 8, per_slope, 0)
    out_ref[...] = out_ref[...] * (1.0 / math.sqrt(SEQ))


def best_of(slopes_and_place, left, mid, right):
    rows, columns = mid.shape
    scratch = pltpu.VMEM((rows, LEFT + columns), jnp.float32)
    return pl.pallas_call(
        best_kernel,
        name="best",
        out_shape=jax.ShapeDtypeStruct((rows - TOP, columns), jnp.float32),
        in_specs=[pl.BlockSpec(memory_space=pltpu.SMEM)] + [pl.BlockSpec(memory_space=pltpu.VMEM)] * 3,
        out_specs=pl.BlockSpec(memory_space=pltpu.VMEM),
        scratch_shapes=[scratch] * 4,
        compiler_params=pltpu.CompilerParams(vmem_limit_bytes=32 << 20),
        cost_estimate=pl.CostEstimate(flops=60 << 20, bytes_accessed=4 << 20, transcendentals=0),
    )(slopes_and_place, left, mid, right)


def local(queries, map_descriptors, slopes):
    ma = lax.axis_index("ma")
    pb = lax.axis_index("pb")
    held, above = gather_queries(queries[0])
    own, other = gather_map(map_descriptors)
    at = []
    for z in range(16):
        at.extend(place(z, ma // 2))
    at.append(pb % 2)
    at = jnp.stack([jnp.asarray(v, jnp.int32) for v in at])
    mid, last, lead = score_tile(at, held, above, own, other)
    left = lax.ppermute(last, "ma", [(i, i + 1) for i in range(31)])
    right = lax.ppermute(lead, "ma", [(i + 1, i) for i in range(31)])
    marks = jnp.concatenate([slopes, ma[None].astype(jnp.int32)])
    return best_of(marks, left, mid, right)[None]


def solution(mesh):
    return jax.shard_map(
        local,
        mesh=mesh,
        in_specs=(P(None, ("pb", "ma"), None), P("ma", "pb"), P()),
        out_specs=P(None, "pb", "ma"),
        check_vma=False,
    )
```

```python
import functools
import math

import jax
import jax.numpy as jnp
from jax import lax
from jax.experimental import pallas as pl
from jax.experimental.pallas import tpu as pltpu
from jax.sharding import PartitionSpec as P

SEQ = 20
RAD = 10
TOP = 32
LEFT = 384
RIGHT = 128
LANES = 128
CHIPS = 8

FAR = (4, 12, 8)
NEAR = (1, 15, 2)


def along_z(step, cross=0):
    return [
        (z * 2 + side, ((z + step) % 16) * 2 + (side ^ cross))
        for z in range(16)
        for side in range(2)
    ]


def gather_queries(queries):
    depth = queries.shape[-1]
    far = jnp.concatenate(
        [queries[None]] + [lax.ppermute(queries[None], "ma", along_z(k)) for k in FAR]
    )
    other = lax.ppermute(far, "ma", along_z(0, 1))
    side = lax.axis_index("ma") % 2
    first = jnp.where(side == 0, far, other)
    second = jnp.where(side == 0, other, far)
    pairs = jnp.concatenate([first, second], axis=1)
    parts = [pairs] + [lax.ppermute(pairs, "ma", along_z(k)) for k in NEAR]
    held = jnp.stack(parts)
    here = lax.axis_index("ma") // 2
    tail = []
    for z in (14, 15):
        near, far_at = place(z, here)
        tail.append(lax.dynamic_slice(held, (near, far_at, 0, 0), (1, 1, 16, depth)))
    tail = jnp.concatenate(tail).reshape(TOP, depth)
    above = lax.ppermute(tail, "pb", [(i, i + 1) for i in range(15)])
    return held, above


def place(z, here):
    delta = (z - here + 16) % 16
    low = delta % 4
    near = jnp.where(low == 0, 0, jnp.where(low == 3, 1, jnp.where(low == 1, 2, 3)))
    back = jnp.where(low == 0, 0, jnp.where(low == 3, -1, jnp.where(low == 1, 1, -2)))
    rest = ((delta - back + 16) % 16) // 4
    far = jnp.where(rest == 0, 0, jnp.where(rest == 3, 1, jnp.where(rest == 1, 2, 3)))
    return near.astype(jnp.int32), far.astype(jnp.int32)


def gather_map(frames):
    groups = [[2 * i + c for i in range(CHIPS)] for c in range(2)]
    copies = jnp.broadcast_to(frames[None], (CHIPS,) + frames.shape)
    own = lax.all_to_all(copies, "pb", 0, 0, axis_index_groups=groups)
    other = lax.ppermute(own, "pb", [(i, i ^ 1) for i in range(16)])
    return own, other


def score_kernel(at_ref, held_ref, above_ref, own_ref, other_ref, out_ref, left_ref, right_ref, rows_ref):
    rows_ref[:TOP] = above_ref[...]
    for z in range(16):
        rows_ref[TOP + 16 * z : TOP + 16 * z + 16] = held_ref[at_ref[2 * z], at_ref[2 * z + 1]]
    core = at_ref[32]
    columns = own_ref.shape[1]
    width = 256

    def block(n, carry):
        begin = pl.multiple_of(n * width, width)
        total = None
        for g in range(CHIPS):
            one = pl.multiple_of((2 * g + core) * LANES, LANES)
            two = pl.multiple_of((2 * g + 1 - core) * LANES, LANES)
            lhs = jnp.concatenate([rows_ref[:, pl.ds(one, LANES)], rows_ref[:, pl.ds(two, LANES)]], axis=1)
            rhs = jnp.concatenate([own_ref[g, pl.ds(begin, width)], other_ref[g, pl.ds(begin, width)]], axis=1)
            part = lax.dot_general(lhs, rhs, (((1,), (1,)), ((), ())), preferred_element_type=jnp.float32)
            total = part if total is None else total + part
        out_ref[:, pl.ds(begin, width)] = total
        return carry

    lax.fori_loop(0, columns // width, block, 0)
    left_ref[...] = out_ref[:, columns - LEFT :]
    right_ref[...] = out_ref[:, :RIGHT]


def score_tile(at, held, above, own, other):
    rows = TOP + 256
    columns = own.shape[1]
    return pl.pallas_call(
        score_kernel,
        name="scores",
        out_shape=(
            jax.ShapeDtypeStruct((rows, columns), jnp.float32),
            jax.ShapeDtypeStruct((rows, LEFT), jnp.float32),
            jax.ShapeDtypeStruct((rows, RIGHT), jnp.float32),
        ),
        in_specs=[pl.BlockSpec(memory_space=pltpu.SMEM)] + [pl.BlockSpec(memory_space=pltpu.VMEM)] * 4,
        out_specs=(pl.BlockSpec(memory_space=pltpu.VMEM),) * 3,
        scratch_shapes=[pltpu.VMEM((rows, 2048), jnp.bfloat16)],
        compiler_params=pltpu.CompilerParams(vmem_limit_bytes=32 << 20),
        cost_estimate=pl.CostEstimate(flops=2 * rows * columns * 2048, bytes_accessed=8 << 20, transcendentals=0),
    )(at, held, above, own, other)


def tile(c):
    return slice(c * LANES, (c + 1) * LANES)


def best_kernel(slopes_ref, left_ref, mid_ref, right_ref, out_ref, split_ref, x_ref, lag_ref, sum_ref, best_ref):
    rows = mid_ref.shape[0]
    columns = mid_ref.shape[1]
    halo = LEFT // LANES
    tiles = halo + columns // LANES
    first_map = slopes_ref[8] == 0

    def source(c):
        if c < halo:
            return left_ref, c
        if c < tiles:
            return mid_ref, c - halo
        return right_ref, c - tiles

    for part in range(6):
        for c in (0, tiles + 2):
            split_ref[part, :, tile(c)] = jnp.zeros((rows, LANES), jnp.bfloat16)

    def split(block, carry):
        take = pl.ds(pl.multiple_of(block * 96, 96), 96)
        for c in range(tiles + 1):
            ref, at = source(c)
            value = ref[take, tile(at)]
            for kind, rest in enumerate((value, value * value)):
                for part in range(3):
                    piece = rest.astype(jnp.bfloat16)
                    split_ref[3 * kind + part, take, tile(c + 1)] = piece
                    rest = rest - piece.astype(jnp.float32)
        return carry

    lax.fori_loop(0, rows // 96, split, 0)
    at_in = lax.broadcasted_iota(jnp.int32, (4 * LANES, 2 * LANES), 0)
    at_out = lax.broadcasted_iota(jnp.int32, (4 * LANES, 2 * LANES), 1) + LANES
    band = jnp.where(jnp.abs(at_in - at_out) <= RAD, 1.0, 0.0).astype(jnp.bfloat16)

    def normalise(block, carry):
        take = pl.ds(pl.multiple_of(block * 96, 96), 96)
        for c in range(0, tiles, 2):
            found = []
            for kind in range(2):
                total = None
                for part in range(3):
                    lhs = split_ref[3 * kind + part, take, c * LANES : (c + 4) * LANES]
                    term = jnp.dot(lhs, band, preferred_element_type=jnp.float32)
                    total = term if total is None else total + term
                found.append(total * (1.0 / (2 * RAD + 1)))
            mean, square = found
            scale = lax.rsqrt(square - mean * mean + 1.0)
            for half in range(2):
                if c + half >= tiles:
                    continue
                ref, at = source(c + half)
                value = (ref[take, tile(at)] - mean[:, tile(half)]) * scale[:, tile(half)]
                if c + half < halo:
                    value = jnp.where(first_map, 0.0, value)
                x_ref[c + half, take] = value
        return carry

    lax.fori_loop(0, rows // 96, normalise, 0)

    steps = SEQ - 1 + 32
    zero = jnp.zeros((8, LANES), jnp.float32)
    for t in range(steps):
        for c in range(halo):
            lag_ref[t, c] = zero
        for c in range(tiles):
            lag_ref[t, c + halo] = x_ref[c, pl.ds(t + TOP - SEQ + 1, 8, stride=32)]
    for index in range(8):
        for c in range(tiles):
            sum_ref[index, c] = zero

    lane = lax.broadcasted_iota(jnp.int32, (8, LANES), 1)

    def step(t, begin, drop, emit):
        best = [None] * tiles
        for index in range(8):
            v = slopes_ref[index]
            by = v
            far = SEQ * v
            whole = far // LANES
            far = far % LANES
            before = zero
            old = None

            def dropped(c):
                return pltpu.roll(lag_ref[t - SEQ, c + halo - whole], far, 1)

            if drop:
                old = dropped(begin - 1)
            for c in range(begin, tiles):
                moved = pltpu.roll(sum_ref[index, c], by, 1)
                total = jnp.where(lane < by, before, moved) + lag_ref[t, c + halo]
                before = moved
                if drop:
                    gone = dropped(c)
                    total = total - jnp.where(lane < far, old, gone)
                    old = gone
                sum_ref[index, c] = total
                if emit and c >= halo:
                    best[c] = total if best[c] is None else jnp.maximum(best[c], total)
        if emit:
            for c in range(halo, tiles):
                best_ref[c - halo, pl.ds(t - SEQ + 1, 8, stride=32)] = best[c] * (1.0 / math.sqrt(SEQ))

    def phase(first, last, begin, drop, emit):
        def body(t, carry):
            step(t, begin, drop, emit)
            return carry

        lax.fori_loop(first, last, body, 0)

    phase(0, SEQ - 1, 0, False, False)
    step(SEQ - 1, 0, False, True)
    phase(SEQ, 34, 0, True, True)
    phase(34, 43, 1, True, True)
    phase(43, steps, 2, True, True)
    for c in range(columns // LANES):
        out_ref[:, tile(c)] = best_ref[c]


def best_of(slopes_and_place, left, mid, right):
    rows, columns = mid.shape
    tiles = (LEFT + columns) // LANES
    return pl.pallas_call(
        best_kernel,
        name="best",
        out_shape=jax.ShapeDtypeStruct((rows - TOP, columns), jnp.float32),
        in_specs=[pl.BlockSpec(memory_space=pltpu.SMEM)] + [pl.BlockSpec(memory_space=pltpu.VMEM)] * 3,
        out_specs=pl.BlockSpec(memory_space=pltpu.VMEM),
        scratch_shapes=[
            pltpu.VMEM((6, rows, (tiles + 3) * LANES), jnp.bfloat16),
            pltpu.VMEM((tiles, rows, LANES), jnp.float32),
            pltpu.VMEM((SEQ + 31, tiles + LEFT // LANES, 8, LANES), jnp.float32),
            pltpu.VMEM((8, tiles, 8, LANES), jnp.float32),
            pltpu.VMEM((columns // LANES, rows - TOP, LANES), jnp.float32),
        ],
        compiler_params=pltpu.CompilerParams(vmem_limit_bytes=32 << 20),
        cost_estimate=pl.CostEstimate(flops=60 << 20, bytes_accessed=4 << 20, transcendentals=0),
    )(slopes_and_place, left, mid, right)


def local(queries, map_descriptors, slopes):
    ma = lax.axis_index("ma")
    pb = lax.axis_index("pb")
    held, above = gather_queries(queries[0])
    own, other = gather_map(map_descriptors)
    at = []
    for z in range(16):
        at.extend(place(z, ma // 2))
    at.append(pb % 2)
    at = jnp.stack([jnp.asarray(v, jnp.int32) for v in at])
    mid, last, lead = score_tile(at, held, above, own, other)
    left = lax.ppermute(last, "ma", [(i, i + 1) for i in range(31)])
    right = lax.ppermute(lead, "ma", [(i + 1, i) for i in range(31)])
    marks = jnp.concatenate([slopes, ma[None].astype(jnp.int32)])
    return best_of(marks, left, mid, right)[None]


def solution(mesh):
    return jax.shard_map(
        local,
        mesh=mesh,
        in_specs=(P(None, ("pb", "ma"), None), P("ma", "pb"), P()),
        out_specs=P(None, "pb", "ma"),
        check_vma=False,
    )
```

```python
import functools
import math

import jax
import jax.numpy as jnp
from jax import lax
from jax.experimental import pallas as pl
from jax.experimental.pallas import tpu as pltpu
from jax.sharding import PartitionSpec as P

SEQ = 20
RAD = 10
TOP = 32
LEFT = 384
LANES = 128
ROWS = TOP + 256
COLUMNS = 1024
HALO = LEFT // LANES
TILES = HALO + COLUMNS // LANES
FIRST, LAST = HALO + 1, TILES - 1
SHIFTS = ((1, 0), (3, 0), (0, 1), (1, 1), (3, 1), (2, 0), (2, 1))


def tile(c):
    return slice(c * LANES, (c + 1) * LANES)


def across(dy, dx, core):
    return [
        (y * 4 + x * 2 + c, (y + dy) % 4 * 4 + (x + dx) % 2 * 2 + (c ^ core))
        for y in range(4)
        for x in range(2)
        for c in range(2)
    ]


def gather(queries, frames):
    depth = queries.shape[-1]
    groups = [[z * 2 + side for z in range(16)] for side in range(2)]
    sides = [(i, i ^ 1) for i in range(32)]
    copies = jnp.broadcast_to(queries[None], (16,) + queries.shape)
    copies, frames = lax.optimization_barrier((copies, frames))
    near = lax.all_to_all(copies, "ma", 0, 0, axis_index_groups=groups)
    own = [frames] + [lax.ppermute(frames, "pb", across(dy, dx, 0)) for dy, dx in SHIFTS]
    own = [jnp.stack(own[:4]), jnp.stack(own[4:])]
    other = [lax.ppermute(part, "pb", across(0, 0, 1)) for part in own]
    far = lax.ppermute(near, "ma", sides)
    near_top = lax.ppermute(near[14:], "pb", [(i, i + 1) for i in range(15)])
    far_top = lax.ppermute(near_top, "ma", sides)
    rows = [v.reshape(-1, depth) for v in (near, far, near_top, far_top)]
    return rows, own + other


def fill_rows(refs, rows_ref):
    at = 0
    for ref in refs:
        rows_ref[at : at + ref.shape[0]] = ref[...]
        at += ref.shape[0]


def products(at_ref, rows_ref, map_refs, begin, width):
    total = None
    for g in range(8):
        one = pl.multiple_of(at_ref[2 * g] * LANES, LANES)
        two = pl.multiple_of(at_ref[2 * g + 1] * LANES, LANES)
        lhs = jnp.concatenate([rows_ref[:, pl.ds(one, LANES)], rows_ref[:, pl.ds(two, LANES)]], axis=1)
        own, other = map_refs[g // 4], map_refs[2 + g // 4]
        rhs = jnp.concatenate([own[g % 4, pl.ds(begin, width)], other[g % 4, pl.ds(begin, width)]], axis=1)
        part = lax.dot_general(lhs, rhs, (((1,), (1,)), ((), ())), preferred_element_type=jnp.float32)
        total = part if total is None else total + part
    return total


def place_rows(side, out_ref, cols, value):
    for r in range(ROWS // 8):
        if r < 32:
            start, far = TOP + 16 * (r % 16), r // 16
        else:
            start, far = 16 * (r % 2), (r - 32) // 2
        start = pl.multiple_of(start + 8 * (side if far == 0 else 1 - side), 8)
        out_ref[pl.ds(start, 8), cols] = value[8 * r : 8 * r + 8]


def edge_kernel(at_ref, *refs):
    row_refs, map_refs, (last_ref, lead_ref, rows_ref) = refs[:4], refs[4:8], refs[8:]
    fill_rows(row_refs, rows_ref)
    side = at_ref[16]
    begin = COLUMNS - LEFT
    for at, width in ((0, 256), (256, 128)):
        value = products(at_ref, rows_ref, map_refs, begin + at, width)
        place_rows(side, last_ref, slice(at, at + width), value)
    place_rows(side, lead_ref, slice(0, LANES), products(at_ref, rows_ref, map_refs, 0, LANES))


def split_tile(split_ref, slot, value):
    for kind, rest in enumerate((value, value * value)):
        for part in range(3):
            piece = rest.astype(jnp.bfloat16)
            split_ref[3 * kind + part, :, tile(slot)] = piece
            if part < 2:
                rest = rest - piece.astype(jnp.float32)


def band_of():
    at_in = lax.broadcasted_iota(jnp.int32, (4 * LANES, 2 * LANES), 0)
    at_out = lax.broadcasted_iota(jnp.int32, (4 * LANES, 2 * LANES), 1) + LANES
    return jnp.where(jnp.abs(at_in - at_out) <= RAD, 1.0, 0.0).astype(jnp.bfloat16)


def contrast_pair(split_ref, slot, band, tiles):
    found = []
    for kind in range(2):
        total = None
        for part in range(3):
            lhs = split_ref[3 * kind + part, :, slot * LANES : (slot + 4) * LANES]
            term = jnp.dot(lhs, band, preferred_element_type=jnp.float32)
            total = term if total is None else total + term
        found.append(total * (1.0 / (2 * RAD + 1)))
    mean, square = found
    scale = lax.rsqrt(square - mean * mean + 1.0)
    return [(v - mean[:, tile(i)]) * scale[:, tile(i)] for i, v in enumerate(tiles)]


def middle_kernel(at_ref, *refs):
    row_refs, map_refs = refs[:4], refs[4:8]
    last_ref, lead_ref, next_ref, inner_ref, rows_ref, mid_ref, split_ref = refs[8:]
    fill_rows(row_refs, rows_ref)
    side = at_ref[16]
    for at in (0, 256):
        value = products(at_ref, rows_ref, map_refs, LANES + at, 256)
        place_rows(side, mid_ref, slice(at, at + 256), value)
    next_ref[...] = mid_ref[:, tile(0)]

    def score(c):
        if c == HALO:
            return lead_ref[...]
        if c < HALO + 5:
            return mid_ref[:, tile(c - HALO - 1)]
        return last_ref[:, tile(c - HALO - 5)]

    for c in range(HALO, TILES):
        split_tile(split_ref, c - HALO, score(c))
    band = band_of()
    for c in range(FIRST, LAST, 2):
        values = contrast_pair(split_ref, c - HALO - 1, band, [score(c), score(c + 1)])
        for half, value in enumerate(values):
            inner_ref[c - FIRST + half] = value


def best_kernel(slopes_ref, left_ref, right_ref, last_ref, lead_ref, next_ref, inner_ref, out_ref, split_ref, x_ref, lag_ref, sum_ref, best_ref):
    first_map = slopes_ref[8] == 0
    empty = jnp.zeros((ROWS, LANES), jnp.bfloat16)
    band = band_of()
    edge = [left_ref[:, tile(c)] for c in range(HALO)] + [lead_ref[...], next_ref[...]]
    for part in range(6):
        split_ref[part, :, tile(0)] = empty
    for c, value in enumerate(edge):
        split_tile(split_ref, c + 1, value)
    for c in (0, 2):
        values = contrast_pair(split_ref, c, band, edge[c : c + 2])
        for half, value in enumerate(values):
            if c + half < HALO:
                value = jnp.where(first_map, 0.0, value)
            x_ref[c + half] = value
    edge = [last_ref[:, tile(1)], last_ref[:, tile(2)], right_ref[...]]
    for part in range(6):
        split_ref[part, :, tile(3)] = empty
    for c, value in enumerate(edge):
        split_tile(split_ref, c, value)
    x_ref[4] = contrast_pair(split_ref, 0, band, edge[1:2])[0]

    def contrast_at(c, row):
        take = pl.ds(row, 8, stride=32)
        if c < FIRST:
            return x_ref[c, take]
        return inner_ref[c - FIRST, take] if c < LAST else x_ref[4, take]

    steps = SEQ - 1 + 32
    zero = jnp.zeros((8, LANES), jnp.float32)
    for t in range(steps):
        for c in range(HALO):
            lag_ref[t, c] = zero
        for c in range(TILES):
            lag_ref[t, c + HALO] = contrast_at(c, t + TOP - SEQ + 1)
    for index in range(8):
        for c in range(TILES):
            sum_ref[index, c] = zero

    lane = lax.broadcasted_iota(jnp.int32, (8, LANES), 1)

    def step(t, begin, drop, emit):
        best = [None] * TILES
        for index in range(8):
            v = slopes_ref[index]
            by = v
            far = SEQ * v
            whole = far // LANES
            far = far % LANES
            before = zero
            old = None

            def dropped(c):
                return pltpu.roll(lag_ref[t - SEQ, c + HALO - whole], far, 1)

            if drop:
                old = dropped(begin - 1)
            for c in range(begin, TILES):
                moved = pltpu.roll(sum_ref[index, c], by, 1)
                total = jnp.where(lane < by, before, moved) + lag_ref[t, c + HALO]
                before = moved
                if drop:
                    gone = dropped(c)
                    total = total - jnp.where(lane < far, old, gone)
                    old = gone
                sum_ref[index, c] = total
                if emit and c >= HALO:
                    best[c] = total if best[c] is None else jnp.maximum(best[c], total)
        if emit:
            for c in range(HALO, TILES):
                best_ref[c - HALO, pl.ds(t - SEQ + 1, 8, stride=32)] = best[c] * (1.0 / math.sqrt(SEQ))

    def phase(first, last, begin, drop, emit):
        def body(t, carry):
            step(t, begin, drop, emit)
            return carry

        lax.fori_loop(first, last, body, 0)

    phase(0, SEQ - 1, 0, False, False)
    step(SEQ - 1, 0, False, True)
    phase(SEQ, 34, 0, True, True)
    phase(34, 43, 1, True, True)
    phase(43, steps, 2, True, True)
    for c in range(COLUMNS // LANES):
        out_ref[:, tile(c)] = best_ref[c]


SMEM = pl.BlockSpec(memory_space=pltpu.SMEM)
VMEM = pl.BlockSpec(memory_space=pltpu.VMEM)
SPLIT = pltpu.VMEM((6, ROWS, 8 * LANES), jnp.bfloat16)


def local(queries, map_descriptors, slopes):
    ma = lax.axis_index("ma")
    pb = lax.axis_index("pb")
    rows, frames = gather(queries[0], map_descriptors)
    y, x, core = pb // 4, pb // 2 % 2, pb % 2
    at = []
    for dy, dx in ((0, 0),) + SHIFTS:
        chip = (y - dy + 4) % 4 * 2 + (x - dx + 2) % 2
        at += [2 * chip + core, 2 * chip + 1 - core]
    at = jnp.stack([jnp.asarray(v, jnp.int32) for v in at + [ma % 2]])
    block = lambda width: jax.ShapeDtypeStruct((ROWS, width), jnp.float32)
    limit = pltpu.CompilerParams(vmem_limit_bytes=40 << 20)
    rows_scratch = pltpu.VMEM((ROWS, 2048), jnp.bfloat16)
    last, lead = pl.pallas_call(
        edge_kernel,
        name="edges",
        out_shape=(block(LEFT), block(LANES)),
        in_specs=[SMEM] + [VMEM] * 8,
        out_specs=(VMEM,) * 2,
        scratch_shapes=[rows_scratch],
        compiler_params=limit,
        cost_estimate=pl.CostEstimate(flops=2 * ROWS * 512 * 2048, bytes_accessed=6 << 20, transcendentals=0),
    )(at, *rows, *frames)
    left = lax.ppermute(last, "ma", [(i, i + 1) for i in range(31)])
    right = lax.ppermute(lead, "ma", [(i + 1, i) for i in range(31)])
    after, inner = pl.pallas_call(
        middle_kernel,
        name="middle",
        out_shape=(block(LANES), jax.ShapeDtypeStruct((LAST - FIRST, ROWS, LANES), jnp.float32)),
        in_specs=[SMEM] + [VMEM] * 10,
        out_specs=(VMEM,) * 2,
        scratch_shapes=[rows_scratch, pltpu.VMEM((ROWS, 512), jnp.float32), SPLIT],
        compiler_params=limit,
        cost_estimate=pl.CostEstimate(flops=8 * ROWS * 512 * 2048, bytes_accessed=16 << 20, transcendentals=0),
    )(at, *rows, *frames, last, lead)
    marks = jnp.concatenate([slopes, ma[None].astype(jnp.int32)])
    best = best_of(marks, left, right, last, lead, after, inner)
    return best[None]


def best_of(marks, left, right, last, lead, after, inner):
    return pl.pallas_call(
        best_kernel,
        name="best",
        out_shape=jax.ShapeDtypeStruct((ROWS - TOP, COLUMNS), jnp.float32),
        in_specs=[SMEM] + [VMEM] * 6,
        out_specs=VMEM,
        scratch_shapes=[
            SPLIT,
            pltpu.VMEM((5, ROWS, LANES), jnp.float32),
            pltpu.VMEM((SEQ + 31, TILES + HALO, 8, LANES), jnp.float32),
            pltpu.VMEM((8, TILES, 8, LANES), jnp.float32),
            pltpu.VMEM((COLUMNS // LANES, ROWS - TOP, LANES), jnp.float32),
        ],
        compiler_params=pltpu.CompilerParams(vmem_limit_bytes=40 << 20),
        cost_estimate=pl.CostEstimate(flops=60 << 20, bytes_accessed=4 << 20, transcendentals=0),
    )(marks, left, right, last, lead, after, inner)


def solution(mesh):
    return jax.shard_map(
        local,
        mesh=mesh,
        in_specs=(P(None, ("pb", "ma"), None), P("ma", "pb"), P()),
        out_specs=P(None, "pb", "ma"),
        check_vma=False,
    )
```

```python
import functools
import math

import jax
import jax.numpy as jnp
from jax import lax
from jax.experimental import pallas as pl
from jax.experimental.pallas import tpu as pltpu
from jax.sharding import PartitionSpec as P

SEQ = 20
RAD = 10
TOP = 32
LEFT = 384
LANES = 128
ROWS = TOP + 256
COLUMNS = 1024
HALO = LEFT // LANES
TILES = HALO + COLUMNS // LANES
FIRST, LAST = HALO + 1, TILES - 1
SHIFTS = ((1, 0), (3, 0), (0, 1), (1, 1), (3, 1), (2, 0), (2, 1))


def tile(c):
    return slice(c * LANES, (c + 1) * LANES)


def across(dy, dx, core):
    return [
        (y * 4 + x * 2 + c, (y + dy) % 4 * 4 + (x + dx) % 2 * 2 + (c ^ core))
        for y in range(4)
        for x in range(2)
        for c in range(2)
    ]


def gather(queries, frames):
    depth = queries.shape[-1]
    groups = [[z * 2 + side for z in range(16)] for side in range(2)]
    sides = [(i, i ^ 1) for i in range(32)]
    copies = jnp.broadcast_to(queries[None], (16,) + queries.shape)
    copies, frames = lax.optimization_barrier((copies, frames))
    near = lax.all_to_all(copies, "ma", 0, 0, axis_index_groups=groups)
    own = [frames] + [lax.ppermute(frames, "pb", across(dy, dx, 0)) for dy, dx in SHIFTS]
    own = [jnp.stack(own[:4]), jnp.stack(own[4:])]
    near_top = lax.ppermute(near[14:], "pb", [(i, i + 1) for i in range(15)])
    parts = [lax.ppermute(near[8:], "ma", sides), lax.ppermute(near[:8], "ma", sides)]
    far_top = lax.ppermute(parts[0][6:], "pb", [(i, i + 1) for i in range(15)])
    own[1], parts[0], near_top = lax.optimization_barrier((own[1], parts[0], near_top))
    far = jnp.concatenate(parts[::-1])
    other = [lax.ppermute(part, "pb", across(0, 0, 1)) for part in own]
    rows = [v.reshape(-1, depth) for v in (near, far, near_top, far_top)]
    return rows, own + other


def fill_rows(refs, rows_ref):
    at = 0
    for ref in refs:
        rows_ref[at : at + ref.shape[0]] = ref[...]
        at += ref.shape[0]


def products(at_ref, rows_ref, map_refs, begin, width):
    total = None
    for g in range(8):
        one = pl.multiple_of(at_ref[2 * g] * LANES, LANES)
        two = pl.multiple_of(at_ref[2 * g + 1] * LANES, LANES)
        lhs = jnp.concatenate([rows_ref[:, pl.ds(one, LANES)], rows_ref[:, pl.ds(two, LANES)]], axis=1)
        own, other = map_refs[g // 4], map_refs[2 + g // 4]
        rhs = jnp.concatenate([own[g % 4, pl.ds(begin, width)], other[g % 4, pl.ds(begin, width)]], axis=1)
        part = lax.dot_general(lhs, rhs, (((1,), (1,)), ((), ())), preferred_element_type=jnp.float32)
        total = part if total is None else total + part
    return total


def place_rows(side, out_ref, cols, value):
    for r in range(ROWS // 8):
        if r < 32:
            start, far = TOP + 16 * (r % 16), r // 16
        else:
            start, far = 16 * (r % 2), (r - 32) // 2
        start = pl.multiple_of(start + 8 * (side if far == 0 else 1 - side), 8)
        out_ref[pl.ds(start, 8), cols] = value[8 * r : 8 * r + 8]


def edge_kernel(at_ref, *refs):
    row_refs, map_refs, (last_ref, lead_ref, rows_ref) = refs[:4], refs[4:8], refs[8:]
    fill_rows(row_refs, rows_ref)
    side = at_ref[16]
    begin = COLUMNS - LEFT
    for at, width in ((0, 256), (256, 128)):
        value = products(at_ref, rows_ref, map_refs, begin + at, width)
        place_rows(side, last_ref, slice(at, at + width), value)
    place_rows(side, lead_ref, slice(0, LANES), products(at_ref, rows_ref, map_refs, 0, LANES))


def split_tile(split_ref, slot, value):
    for kind, rest in enumerate((value, value * value)):
        for part in range(3):
            piece = rest.astype(jnp.bfloat16)
            split_ref[3 * kind + part, :, tile(slot)] = piece
            if part < 2:
                rest = rest - piece.astype(jnp.float32)


def band_of():
    at_in = lax.broadcasted_iota(jnp.int32, (4 * LANES, 2 * LANES), 0)
    at_out = lax.broadcasted_iota(jnp.int32, (4 * LANES, 2 * LANES), 1) + LANES
    return jnp.where(jnp.abs(at_in - at_out) <= RAD, 1.0, 0.0).astype(jnp.bfloat16)


def contrast_pair(split_ref, slot, band, tiles):
    found = []
    for kind in range(2):
        total = None
        for part in range(3):
            lhs = split_ref[3 * kind + part, :, slot * LANES : (slot + 4) * LANES]
            term = jnp.dot(lhs, band, preferred_element_type=jnp.float32)
            total = term if total is None else total + term
        found.append(total * (1.0 / (2 * RAD + 1)))
    mean, square = found
    scale = lax.rsqrt(square - mean * mean + 1.0)
    return [(v - mean[:, tile(i)]) * scale[:, tile(i)] for i, v in enumerate(tiles)]


def middle_kernel(at_ref, *refs):
    row_refs, map_refs = refs[:4], refs[4:8]
    last_ref, lead_ref, next_ref, inner_ref, rows_ref, mid_ref, split_ref = refs[8:]
    fill_rows(row_refs, rows_ref)
    side = at_ref[16]
    for at in (0, 256):
        value = products(at_ref, rows_ref, map_refs, LANES + at, 256)
        place_rows(side, mid_ref, slice(at, at + 256), value)
    next_ref[...] = mid_ref[:, tile(0)]

    def score(c):
        if c == HALO:
            return lead_ref[...]
        if c < HALO + 5:
            return mid_ref[:, tile(c - HALO - 1)]
        return last_ref[:, tile(c - HALO - 5)]

    for c in range(HALO, TILES):
        split_tile(split_ref, c - HALO, score(c))
    band = band_of()
    for c in range(FIRST, LAST, 2):
        values = contrast_pair(split_ref, c - HALO - 1, band, [score(c), score(c + 1)])
        for half, value in enumerate(values):
            inner_ref[c - FIRST + half] = value


def best_kernel(slopes_ref, left_ref, right_ref, last_ref, lead_ref, next_ref, inner_ref, out_ref, split_ref, x_ref, lag_ref, sum_ref, best_ref):
    first_map = slopes_ref[8] == 0
    empty = jnp.zeros((ROWS, LANES), jnp.bfloat16)
    band = band_of()
    edge = [left_ref[:, tile(c)] for c in range(HALO)] + [lead_ref[...], next_ref[...]]
    for part in range(6):
        split_ref[part, :, tile(0)] = empty
    for c, value in enumerate(edge):
        split_tile(split_ref, c + 1, value)
    for c in (0, 2):
        values = contrast_pair(split_ref, c, band, edge[c : c + 2])
        for half, value in enumerate(values):
            if c + half < HALO:
                value = jnp.where(first_map, 0.0, value)
            x_ref[c + half] = value
    edge = [last_ref[:, tile(1)], last_ref[:, tile(2)], right_ref[...]]
    for part in range(6):
        split_ref[part, :, tile(3)] = empty
    for c, value in enumerate(edge):
        split_tile(split_ref, c, value)
    x_ref[4] = contrast_pair(split_ref, 0, band, edge[1:2])[0]

    def contrast_at(c, row):
        take = pl.ds(row, 8, stride=32)
        if c < FIRST:
            return x_ref[c, take]
        return inner_ref[c - FIRST, take] if c < LAST else x_ref[4, take]

    steps = SEQ - 1 + 32
    zero = jnp.zeros((8, LANES), jnp.float32)
    for t in range(steps):
        for c in range(HALO):
            lag_ref[t, c] = zero
        for c in range(TILES):
            lag_ref[t, c + HALO] = contrast_at(c, t + TOP - SEQ + 1)
    for index in range(8):
        for c in range(TILES):
            sum_ref[index, c] = zero

    lane = lax.broadcasted_iota(jnp.int32, (8, LANES), 1)

    def step(t, begin, drop, emit):
        best = [None] * TILES
        for index in range(8):
            v = slopes_ref[index]
            by = v
            far = SEQ * v
            whole = far // LANES
            far = far % LANES
            before = zero
            old = None

            def dropped(c):
                return pltpu.roll(lag_ref[t - SEQ, c + HALO - whole], far, 1)

            if drop:
                old = dropped(begin - 1)
            for c in range(begin, TILES):
                moved = pltpu.roll(sum_ref[index, c], by, 1)
                total = jnp.where(lane < by, before, moved) + lag_ref[t, c + HALO]
                before = moved
                if drop:
                    gone = dropped(c)
                    total = total - jnp.where(lane < far, old, gone)
                    old = gone
                sum_ref[index, c] = total
                if emit and c >= HALO:
                    best[c] = total if best[c] is None else jnp.maximum(best[c], total)
        if emit:
            for c in range(HALO, TILES):
                best_ref[c - HALO, pl.ds(t - SEQ + 1, 8, stride=32)] = best[c] * (1.0 / math.sqrt(SEQ))

    def phase(first, last, begin, drop, emit):
        def body(t, carry):
            step(t, begin, drop, emit)
            return carry

        lax.fori_loop(first, last, body, 0, unroll=2)

    phase(0, SEQ - 1, 0, False, False)
    step(SEQ - 1, 0, False, True)
    phase(SEQ, 34, 0, True, True)
    phase(34, 43, 1, True, True)
    phase(43, steps, 2, True, True)
    for c in range(COLUMNS // LANES):
        out_ref[:, tile(c)] = best_ref[c]


SMEM = pl.BlockSpec(memory_space=pltpu.SMEM)
VMEM = pl.BlockSpec(memory_space=pltpu.VMEM)
SPLIT = pltpu.VMEM((6, ROWS, 8 * LANES), jnp.bfloat16)


def local(queries, map_descriptors, slopes):
    ma = lax.axis_index("ma")
    pb = lax.axis_index("pb")
    rows, frames = gather(queries[0], map_descriptors)
    y, x, core = pb // 4, pb // 2 % 2, pb % 2
    at = []
    for dy, dx in ((0, 0),) + SHIFTS:
        chip = (y - dy + 4) % 4 * 2 + (x - dx + 2) % 2
        at += [2 * chip + core, 2 * chip + 1 - core]
    at = jnp.stack([jnp.asarray(v, jnp.int32) for v in at + [ma % 2]])
    block = lambda width: jax.ShapeDtypeStruct((ROWS, width), jnp.float32)
    limit = pltpu.CompilerParams(vmem_limit_bytes=40 << 20)
    rows_scratch = pltpu.VMEM((ROWS, 2048), jnp.bfloat16)
    last, lead = pl.pallas_call(
        edge_kernel,
        name="edges",
        out_shape=(block(LEFT), block(LANES)),
        in_specs=[SMEM] + [VMEM] * 8,
        out_specs=(VMEM,) * 2,
        scratch_shapes=[rows_scratch],
        compiler_params=limit,
        cost_estimate=pl.CostEstimate(flops=2 * ROWS * 512 * 2048, bytes_accessed=6 << 20, transcendentals=0),
    )(at, *rows, *frames)
    left = lax.ppermute(last, "ma", [(i, i + 1) for i in range(31)])
    right = lax.ppermute(lead, "ma", [(i + 1, i) for i in range(31)])
    after, inner = pl.pallas_call(
        middle_kernel,
        name="middle",
        out_shape=(block(LANES), jax.ShapeDtypeStruct((LAST - FIRST, ROWS, LANES), jnp.float32)),
        in_specs=[SMEM] + [VMEM] * 10,
        out_specs=(VMEM,) * 2,
        scratch_shapes=[rows_scratch, pltpu.VMEM((ROWS, 512), jnp.float32), SPLIT],
        compiler_params=limit,
        cost_estimate=pl.CostEstimate(flops=8 * ROWS * 512 * 2048, bytes_accessed=16 << 20, transcendentals=0),
    )(at, *rows, *frames, last, lead)
    marks = jnp.concatenate([slopes, ma[None].astype(jnp.int32)])
    best = best_of(marks, left, right, last, lead, after, inner)
    return best[None]


def best_of(marks, left, right, last, lead, after, inner):
    return pl.pallas_call(
        best_kernel,
        name="best",
        out_shape=jax.ShapeDtypeStruct((ROWS - TOP, COLUMNS), jnp.float32),
        in_specs=[SMEM] + [VMEM] * 6,
        out_specs=VMEM,
        scratch_shapes=[
            SPLIT,
            pltpu.VMEM((5, ROWS, LANES), jnp.float32),
            pltpu.VMEM((SEQ + 31, TILES + HALO, 8, LANES), jnp.float32),
            pltpu.VMEM((8, TILES, 8, LANES), jnp.float32),
            pltpu.VMEM((COLUMNS // LANES, ROWS - TOP, LANES), jnp.float32),
        ],
        compiler_params=pltpu.CompilerParams(vmem_limit_bytes=40 << 20),
        cost_estimate=pl.CostEstimate(flops=60 << 20, bytes_accessed=4 << 20, transcendentals=0),
    )(marks, left, right, last, lead, after, inner)


def solution(mesh):
    return jax.shard_map(
        local,
        mesh=mesh,
        in_specs=(P(None, ("pb", "ma"), None), P("ma", "pb"), P()),
        out_specs=P(None, "pb", "ma"),
        check_vma=False,
    )
```

```python
import functools
import math

import jax
import jax.numpy as jnp
from jax import lax
from jax.experimental import pallas as pl
from jax.experimental.pallas import tpu as pltpu
from jax.sharding import PartitionSpec as P

SEQ = 20
RAD = 10
TOP = 32
LEFT = 384
LANES = 128
ROWS = TOP + 256
COLUMNS = 1024
THIRD = ROWS // 3
PACK = 40
HALO = LEFT // LANES
TILES = HALO + COLUMNS // LANES
FIRST, LAST = HALO + 1, TILES - 1
SHIFTS = ((1, 0), (1, 1), (3, 1), (3, 0), (2, 0), (2, 1), (0, 1))


def tile(c):
    return slice(c * LANES, (c + 1) * LANES)


def across(dy, dx, core):
    return [
        (y * 4 + x * 2 + c, (y + dy) % 4 * 4 + (x + dx) % 2 * 2 + (c ^ core))
        for y in range(4)
        for x in range(2)
        for c in range(2)
    ]


def gather(queries, frames):
    depth = queries.shape[-1]
    groups = [[z * 2 + side for z in range(16)] for side in range(2)]
    sides = [(i, i ^ 1) for i in range(32)]
    copies = jnp.broadcast_to(queries[None], (16,) + queries.shape)
    copies, frames = lax.optimization_barrier((copies, frames))
    near = lax.all_to_all(copies, "ma", 0, 0, axis_index_groups=groups)
    own = [frames] + [lax.ppermute(frames, "pb", across(dy, dx, 0)) for dy, dx in SHIFTS]
    own = [jnp.stack(own[:4]), jnp.stack(own[4:])]
    near_top = lax.ppermute(near[14:], "pb", [(i, i + 1) for i in range(15)])
    parts = [lax.ppermute(near[8:], "ma", sides), lax.ppermute(near[:8], "ma", sides)]
    far_top = lax.ppermute(parts[0][6:], "pb", [(i, i + 1) for i in range(15)])
    own[1], parts[0], near_top = lax.optimization_barrier((own[1], parts[0], near_top))
    far = jnp.concatenate(parts[::-1])
    other = [lax.ppermute(part, "pb", across(0, 0, 1)) for part in own]
    rows = [v.reshape(-1, depth) for v in (near, far, near_top, far_top)]
    return rows, own + other


def fill_rows(refs, rows_ref):
    at = 0
    for ref in refs:
        rows_ref[at : at + ref.shape[0]] = ref[...]
        at += ref.shape[0]


def products(at_ref, rows_ref, map_refs, begin, width):
    total = None
    for g in range(8):
        one = pl.multiple_of(at_ref[2 * g] * LANES, LANES)
        two = pl.multiple_of(at_ref[2 * g + 1] * LANES, LANES)
        lhs = jnp.concatenate([rows_ref[:, pl.ds(one, LANES)], rows_ref[:, pl.ds(two, LANES)]], axis=1)
        own, other = map_refs[g // 4], map_refs[2 + g // 4]
        rhs = jnp.concatenate([own[g % 4, pl.ds(begin, width)], other[g % 4, pl.ds(begin, width)]], axis=1)
        part = lax.dot_general(lhs, rhs, (((1,), (1,)), ((), ())), preferred_element_type=jnp.float32)
        total = part if total is None else total + part
    return total


def place_rows(side, out_ref, cols, value):
    for r in range(ROWS // 8):
        if r < 32:
            start, far = TOP + 16 * (r % 16), r // 16
        else:
            start, far = 16 * (r % 2), (r - 32) // 2
        start = pl.multiple_of(start + 8 * (side if far == 0 else 1 - side), 8)
        out_ref[pl.ds(start, 8), cols] = value[8 * r : 8 * r + 8]


def packed(ref, cols, first):
    lane = lax.broadcasted_iota(jnp.int32, (THIRD, LANES), 1)
    parts = [
        pltpu.roll(ref[g * THIRD : (g + 1) * THIRD, cols], (PACK * g - first) % LANES, 1)
        for g in range(3)
    ]
    return jnp.where(lane < PACK, parts[0], jnp.where(lane < 2 * PACK, parts[1], parts[2]))


def unpacked(value, first):
    parts = [pltpu.roll(value, (first - PACK * g) % LANES, 1) for g in range(3)]
    return jnp.concatenate(parts)


def edge_kernel(at_ref, *refs):
    row_refs, map_refs = refs[:4], refs[4:8]
    last_ref, lead_ref, left_ref, right_ref, rows_ref = refs[8:]
    fill_rows(row_refs, rows_ref)
    side = at_ref[16]
    begin = COLUMNS - LEFT
    for at, width in ((0, 256), (256, 128)):
        value = products(at_ref, rows_ref, map_refs, begin + at, width)
        place_rows(side, last_ref, slice(at, at + width), value)
    place_rows(side, lead_ref, slice(0, LANES), products(at_ref, rows_ref, map_refs, 0, LANES))
    left_ref[:ROWS] = last_ref[:, tile(1)]
    left_ref[ROWS : 2 * ROWS] = last_ref[:, tile(2)]
    left_ref[2 * ROWS :] = packed(last_ref, tile(0), LANES - PACK)
    right_ref[...] = packed(lead_ref, tile(0), 0)


def split_tile(split_ref, slot, value):
    for kind, rest in enumerate((value, value * value)):
        for part in range(3):
            piece = rest.astype(jnp.bfloat16)
            split_ref[3 * kind + part, :, tile(slot)] = piece
            if part < 2:
                rest = rest - piece.astype(jnp.float32)


def band_of():
    at_in = lax.broadcasted_iota(jnp.int32, (4 * LANES, 2 * LANES), 0)
    at_out = lax.broadcasted_iota(jnp.int32, (4 * LANES, 2 * LANES), 1) + LANES
    return jnp.where(jnp.abs(at_in - at_out) <= RAD, 1.0, 0.0).astype(jnp.bfloat16)


def contrast_pair(split_ref, slot, band, tiles):
    found = []
    for kind in range(2):
        total = None
        for part in range(3):
            lhs = split_ref[3 * kind + part, :, slot * LANES : (slot + 4) * LANES]
            term = jnp.dot(lhs, band, preferred_element_type=jnp.float32)
            total = term if total is None else total + term
        found.append(total * (1.0 / (2 * RAD + 1)))
    mean, square = found
    scale = lax.rsqrt(square - mean * mean + 1.0)
    return [(v - mean[:, tile(i)]) * scale[:, tile(i)] for i, v in enumerate(tiles)]


def middle_kernel(at_ref, *refs):
    row_refs, map_refs = refs[:4], refs[4:8]
    last_ref, lead_ref, next_ref, inner_ref, rows_ref, mid_ref, split_ref = refs[8:]
    fill_rows(row_refs, rows_ref)
    side = at_ref[16]
    for at in (0, 256):
        value = products(at_ref, rows_ref, map_refs, LANES + at, 256)
        place_rows(side, mid_ref, slice(at, at + 256), value)
    next_ref[...] = mid_ref[:, tile(0)]

    def score(c):
        if c == HALO:
            return lead_ref[...]
        if c < HALO + 5:
            return mid_ref[:, tile(c - HALO - 1)]
        return last_ref[:, tile(c - HALO - 5)]

    for c in range(HALO, TILES):
        split_tile(split_ref, c - HALO, score(c))
    band = band_of()
    for c in range(FIRST, LAST, 2):
        values = contrast_pair(split_ref, c - HALO - 1, band, [score(c), score(c + 1)])
        for half, value in enumerate(values):
            inner_ref[c - FIRST + half] = value


def best_kernel(slopes_ref, left_ref, right_ref, last_ref, lead_ref, next_ref, inner_ref, out_ref, split_ref, x_ref, lag_ref, sum_ref, best_ref):
    first_map = slopes_ref[8] == 0
    empty = jnp.zeros((ROWS, LANES), jnp.bfloat16)
    band = band_of()
    farthest = unpacked(left_ref[2 * ROWS :], LANES - PACK)
    edge = [farthest, left_ref[:ROWS], left_ref[ROWS : 2 * ROWS], lead_ref[...], next_ref[...]]
    for part in range(6):
        split_ref[part, :, tile(0)] = empty
    for c, value in enumerate(edge):
        split_tile(split_ref, c + 1, value)
    for c in (0, 2):
        values = contrast_pair(split_ref, c, band, edge[c : c + 2])
        for half, value in enumerate(values):
            if c + half < HALO:
                value = jnp.where(first_map, 0.0, value)
            x_ref[c + half] = value
    edge = [last_ref[:, tile(1)], last_ref[:, tile(2)], unpacked(right_ref[...], 0)]
    for part in range(6):
        split_ref[part, :, tile(3)] = empty
    for c, value in enumerate(edge):
        split_tile(split_ref, c, value)
    x_ref[4] = contrast_pair(split_ref, 0, band, edge[1:2])[0]

    def contrast_at(c, row):
        take = pl.ds(row, 8, stride=32)
        if c < FIRST:
            return x_ref[c, take]
        return inner_ref[c - FIRST, take] if c < LAST else x_ref[4, take]

    steps = SEQ - 1 + 32
    zero = jnp.zeros((8, LANES), jnp.float32)
    for t in range(steps):
        for c in range(HALO):
            lag_ref[t, c] = zero
        for c in range(TILES):
            lag_ref[t, c + HALO] = contrast_at(c, t + TOP - SEQ + 1)
    for index in range(8):
        for c in range(TILES):
            sum_ref[index, c] = zero

    lane = lax.broadcasted_iota(jnp.int32, (8, LANES), 1)

    def step(t, begin, drop, emit):
        best = [None] * TILES
        for index in range(8):
            v = slopes_ref[index]
            by = v
            far = SEQ * v
            whole = far // LANES
            far = far % LANES
            before = zero
            old = None

            def dropped(c):
                return pltpu.roll(lag_ref[t - SEQ, c + HALO - whole], far, 1)

            if drop:
                old = dropped(begin - 1)
            for c in range(begin, TILES):
                moved = pltpu.roll(sum_ref[index, c], by, 1)
                total = jnp.where(lane < by, before, moved) + lag_ref[t, c + HALO]
                before = moved
                if drop:
                    gone = dropped(c)
                    total = total - jnp.where(lane < far, old, gone)
                    old = gone
                sum_ref[index, c] = total
                if emit and c >= HALO:
                    best[c] = total if best[c] is None else jnp.maximum(best[c], total)
        if emit:
            for c in range(HALO, TILES):
                best_ref[c - HALO, pl.ds(t - SEQ + 1, 8, stride=32)] = best[c] * (1.0 / math.sqrt(SEQ))

    def phase(first, last, begin, drop, emit):
        def body(t, carry):
            step(t, begin, drop, emit)
            return carry

        lax.fori_loop(first, last, body, 0, unroll=2)

    phase(0, SEQ - 1, 0, False, False)
    step(SEQ - 1, 0, False, True)
    phase(SEQ, 34, 0, True, True)
    phase(34, 43, 1, True, True)
    phase(43, steps, 2, True, True)
    for c in range(COLUMNS // LANES):
        out_ref[:, tile(c)] = best_ref[c]


SMEM = pl.BlockSpec(memory_space=pltpu.SMEM)
VMEM = pl.BlockSpec(memory_space=pltpu.VMEM)
SPLIT = pltpu.VMEM((6, ROWS, 8 * LANES), jnp.bfloat16)


def local(queries, map_descriptors, slopes):
    ma = lax.axis_index("ma")
    pb = lax.axis_index("pb")
    rows, frames = gather(queries[0], map_descriptors)
    y, x, core = pb // 4, pb // 2 % 2, pb % 2
    at = []
    for dy, dx in ((0, 0),) + SHIFTS:
        chip = (y - dy + 4) % 4 * 2 + (x - dx + 2) % 2
        at += [2 * chip + core, 2 * chip + 1 - core]
    at = jnp.stack([jnp.asarray(v, jnp.int32) for v in at + [ma % 2]])
    block = lambda width: jax.ShapeDtypeStruct((ROWS, width), jnp.float32)
    limit = pltpu.CompilerParams(vmem_limit_bytes=40 << 20)
    rows_scratch = pltpu.VMEM((ROWS, 2048), jnp.bfloat16)
    lines = lambda count: jax.ShapeDtypeStruct((count, LANES), jnp.float32)
    last, lead, left, right = pl.pallas_call(
        edge_kernel,
        name="edges",
        out_shape=(block(LEFT), block(LANES), lines(2 * ROWS + THIRD), lines(THIRD)),
        in_specs=[SMEM] + [VMEM] * 8,
        out_specs=(VMEM,) * 4,
        scratch_shapes=[rows_scratch],
        compiler_params=limit,
        cost_estimate=pl.CostEstimate(flops=2 * ROWS * 512 * 2048, bytes_accessed=6 << 20, transcendentals=0),
    )(at, *rows, *frames)
    left = lax.ppermute(left, "ma", [(i, i + 1) for i in range(31)])
    right = lax.ppermute(right, "ma", [(i + 1, i) for i in range(31)])
    after, inner = pl.pallas_call(
        middle_kernel,
        name="middle",
        out_shape=(block(LANES), jax.ShapeDtypeStruct((LAST - FIRST, ROWS, LANES), jnp.float32)),
        in_specs=[SMEM] + [VMEM] * 10,
        out_specs=(VMEM,) * 2,
        scratch_shapes=[rows_scratch, pltpu.VMEM((ROWS, 512), jnp.float32), SPLIT],
        compiler_params=limit,
        cost_estimate=pl.CostEstimate(flops=8 * ROWS * 512 * 2048, bytes_accessed=16 << 20, transcendentals=0),
    )(at, *rows, *frames, last, lead)
    marks = jnp.concatenate([slopes, ma[None].astype(jnp.int32)])
    best = best_of(marks, left, right, last, lead, after, inner)
    return best[None]


def best_of(marks, left, right, last, lead, after, inner):
    return pl.pallas_call(
        best_kernel,
        name="best",
        out_shape=jax.ShapeDtypeStruct((ROWS - TOP, COLUMNS), jnp.float32),
        in_specs=[SMEM] + [VMEM] * 6,
        out_specs=VMEM,
        scratch_shapes=[
            SPLIT,
            pltpu.VMEM((5, ROWS, LANES), jnp.float32),
            pltpu.VMEM((SEQ + 31, TILES + HALO, 8, LANES), jnp.float32),
            pltpu.VMEM((8, TILES, 8, LANES), jnp.float32),
            pltpu.VMEM((COLUMNS // LANES, ROWS - TOP, LANES), jnp.float32),
        ],
        compiler_params=pltpu.CompilerParams(vmem_limit_bytes=40 << 20),
        cost_estimate=pl.CostEstimate(flops=60 << 20, bytes_accessed=4 << 20, transcendentals=0),
    )(marks, left, right, last, lead, after, inner)


def solution(mesh):
    return jax.shard_map(
        local,
        mesh=mesh,
        in_specs=(P(None, ("pb", "ma"), None), P("ma", "pb"), P()),
        out_specs=P(None, "pb", "ma"),
        check_vma=False,
    )
```

```python
import functools
import math

import jax
import jax.numpy as jnp
from jax import lax
from jax.experimental import pallas as pl
from jax.experimental.pallas import tpu as pltpu
from jax.sharding import PartitionSpec as P

SEQ = 20
RAD = 10
TOP = 32
LEFT = 384
LANES = 128
ROWS = TOP + 256
COLUMNS = 1024
THIRD = ROWS // 3
PACK = 40
HALO = LEFT // LANES
TILES = HALO + COLUMNS // LANES
FIRST, LAST = HALO + 1, TILES - 1
SHIFTS = ((1, 0), (3, 0), (0, 1), (1, 1), (3, 1), (2, 0), (2, 1))


def tile(c):
    return slice(c * LANES, (c + 1) * LANES)


def across(dy, dx, core):
    return [
        (y * 4 + x * 2 + c, (y + dy) % 4 * 4 + (x + dx) % 2 * 2 + (c ^ core))
        for y in range(4)
        for x in range(2)
        for c in range(2)
    ]


def gather(queries, frames):
    depth = queries.shape[-1]
    groups = [[z * 2 + side for z in range(16)] for side in range(2)]
    sides = [(i, i ^ 1) for i in range(32)]
    copies = jnp.broadcast_to(queries[None], (16,) + queries.shape)
    copies, frames = lax.optimization_barrier((copies, frames))
    near = lax.all_to_all(copies, "ma", 0, 0, axis_index_groups=groups)
    own = [frames] + [lax.ppermute(frames, "pb", across(dy, dx, 0)) for dy, dx in SHIFTS]
    own = [jnp.stack(own[:4]), jnp.stack(own[4:])]
    near_top = lax.ppermute(near[14:], "pb", [(i, i + 1) for i in range(15)])
    parts = [lax.ppermute(near[8:], "ma", sides), lax.ppermute(near[:8], "ma", sides)]
    far_top = lax.ppermute(parts[0][6:], "pb", [(i, i + 1) for i in range(15)])
    own[1], parts[0], near_top = lax.optimization_barrier((own[1], parts[0], near_top))
    far = jnp.concatenate(parts[::-1])
    other = [lax.ppermute(part, "pb", across(0, 0, 1)) for part in own]
    rows = [v.reshape(-1, depth) for v in (near, far, near_top, far_top)]
    return rows, own + other


def fill_rows(refs, rows_ref):
    at = 0
    for ref in refs:
        rows_ref[at : at + ref.shape[0]] = ref[...]
        at += ref.shape[0]


def products(at_ref, rows_ref, map_refs, begin, width):
    total = None
    for g in range(8):
        one = pl.multiple_of(at_ref[2 * g] * LANES, LANES)
        two = pl.multiple_of(at_ref[2 * g + 1] * LANES, LANES)
        lhs = jnp.concatenate([rows_ref[:, pl.ds(one, LANES)], rows_ref[:, pl.ds(two, LANES)]], axis=1)
        own, other = map_refs[g // 4], map_refs[2 + g // 4]
        rhs = jnp.concatenate([own[g % 4, pl.ds(begin, width)], other[g % 4, pl.ds(begin, width)]], axis=1)
        part = lax.dot_general(lhs, rhs, (((1,), (1,)), ((), ())), preferred_element_type=jnp.float32)
        total = part if total is None else total + part
    return total


def place_rows(side, out_ref, cols, value):
    for r in range(ROWS // 8):
        if r < 32:
            start, far = TOP + 16 * (r % 16), r // 16
        else:
            start, far = 16 * (r % 2), (r - 32) // 2
        start = pl.multiple_of(start + 8 * (side if far == 0 else 1 - side), 8)
        out_ref[pl.ds(start, 8), cols] = value[8 * r : 8 * r + 8]


def packed(ref, cols, first):
    lane = lax.broadcasted_iota(jnp.int32, (THIRD, LANES), 1)
    parts = [
        pltpu.roll(ref[g * THIRD : (g + 1) * THIRD, cols], (PACK * g - first) % LANES, 1)
        for g in range(3)
    ]
    return jnp.where(lane < PACK, parts[0], jnp.where(lane < 2 * PACK, parts[1], parts[2]))


def unpacked(value, first):
    parts = [pltpu.roll(value, (first - PACK * g) % LANES, 1) for g in range(3)]
    return jnp.concatenate(parts)


def edge_kernel(at_ref, *refs):
    row_refs, map_refs = refs[:4], refs[4:8]
    last_ref, lead_ref, left_ref, right_ref, rows_ref = refs[8:]
    fill_rows(row_refs, rows_ref)
    side = at_ref[16]
    begin = COLUMNS - LEFT
    for at, width in ((0, 256), (256, 128)):
        value = products(at_ref, rows_ref, map_refs, begin + at, width)
        place_rows(side, last_ref, slice(at, at + width), value)
    place_rows(side, lead_ref, slice(0, LANES), products(at_ref, rows_ref, map_refs, 0, LANES))
    left_ref[:ROWS] = last_ref[:, tile(1)]
    left_ref[ROWS : 2 * ROWS] = last_ref[:, tile(2)]
    left_ref[2 * ROWS :] = packed(last_ref, tile(0), LANES - PACK)
    right_ref[...] = packed(lead_ref, tile(0), 0)


def split_tile(split_ref, slot, value):
    for kind, rest in enumerate((value, value * value)):
        for part in range(3):
            piece = rest.astype(jnp.bfloat16)
            split_ref[3 * kind + part, :, tile(slot)] = piece
            if part < 2:
                rest = rest - piece.astype(jnp.float32)


def band_of():
    at_in = lax.broadcasted_iota(jnp.int32, (4 * LANES, 2 * LANES), 0)
    at_out = lax.broadcasted_iota(jnp.int32, (4 * LANES, 2 * LANES), 1) + LANES
    return jnp.where(jnp.abs(at_in - at_out) <= RAD, 1.0, 0.0).astype(jnp.bfloat16)


def contrast_pair(split_ref, slot, band, tiles):
    found = []
    for kind in range(2):
        total = None
        for part in range(3):
            lhs = split_ref[3 * kind + part, :, slot * LANES : (slot + 4) * LANES]
            term = jnp.dot(lhs, band, preferred_element_type=jnp.float32)
            total = term if total is None else total + term
        found.append(total * (1.0 / (2 * RAD + 1)))
    mean, square = found
    scale = lax.rsqrt(square - mean * mean + 1.0)
    return [(v - mean[:, tile(i)]) * scale[:, tile(i)] for i, v in enumerate(tiles)]


def middle_kernel(at_ref, *refs):
    row_refs, map_refs = refs[:4], refs[4:8]
    last_ref, lead_ref, next_ref, inner_ref, rows_ref, mid_ref, split_ref = refs[8:]
    fill_rows(row_refs, rows_ref)
    side = at_ref[16]
    for at in (0, 256):
        value = products(at_ref, rows_ref, map_refs, LANES + at, 256)
        place_rows(side, mid_ref, slice(at, at + 256), value)
    next_ref[...] = mid_ref[:, tile(0)]

    def score(c):
        if c == HALO:
            return lead_ref[...]
        if c < HALO + 5:
            return mid_ref[:, tile(c - HALO - 1)]
        return last_ref[:, tile(c - HALO - 5)]

    for c in range(HALO, TILES):
        split_tile(split_ref, c - HALO, score(c))
    band = band_of()
    for c in range(FIRST, LAST, 2):
        values = contrast_pair(split_ref, c - HALO - 1, band, [score(c), score(c + 1)])
        for half, value in enumerate(values):
            inner_ref[c - FIRST + half] = value


def best_kernel(slopes_ref, left_ref, right_ref, last_ref, lead_ref, next_ref, inner_ref, out_ref, split_ref, x_ref, lag_ref, sum_ref, best_ref):
    first_map = slopes_ref[8] == 0
    empty = jnp.zeros((ROWS, LANES), jnp.bfloat16)
    band = band_of()
    farthest = unpacked(left_ref[2 * ROWS :], LANES - PACK)
    edge = [farthest, left_ref[:ROWS], left_ref[ROWS : 2 * ROWS], lead_ref[...], next_ref[...]]
    for part in range(6):
        split_ref[part, :, tile(0)] = empty
    for c, value in enumerate(edge):
        split_tile(split_ref, c + 1, value)
    for c in (0, 2):
        values = contrast_pair(split_ref, c, band, edge[c : c + 2])
        for half, value in enumerate(values):
            if c + half < HALO:
                value = jnp.where(first_map, 0.0, value)
            x_ref[c + half] = value
    edge = [last_ref[:, tile(1)], last_ref[:, tile(2)], unpacked(right_ref[...], 0)]
    for part in range(6):
        split_ref[part, :, tile(3)] = empty
    for c, value in enumerate(edge):
        split_tile(split_ref, c, value)
    x_ref[4] = contrast_pair(split_ref, 0, band, edge[1:2])[0]

    def contrast_at(c, row):
        take = pl.ds(row, 8, stride=32)
        if c < FIRST:
            return x_ref[c, take]
        return inner_ref[c - FIRST, take] if c < LAST else x_ref[4, take]

    steps = SEQ - 1 + 32
    zero = jnp.zeros((8, LANES), jnp.float32)
    for t in range(steps):
        for c in range(HALO):
            lag_ref[t, c] = zero
        for c in range(TILES):
            lag_ref[t, c + HALO] = contrast_at(c, t + TOP - SEQ + 1)
    for index in range(8):
        for c in range(TILES):
            sum_ref[index, c] = zero

    lane = lax.broadcasted_iota(jnp.int32, (8, LANES), 1)

    def step(t, begin, drop, emit):
        best = [None] * TILES
        for index in range(8):
            v = slopes_ref[index]
            by = v
            far = SEQ * v
            whole = far // LANES
            far = far % LANES
            before = zero
            old = None

            def dropped(c):
                return pltpu.roll(lag_ref[t - SEQ, c + HALO - whole], far, 1)

            if drop:
                old = dropped(begin - 1)
            for c in range(begin, TILES):
                moved = pltpu.roll(sum_ref[index, c], by, 1)
                total = jnp.where(lane < by, before, moved) + lag_ref[t, c + HALO]
                before = moved
                if drop:
                    gone = dropped(c)
                    total = total - jnp.where(lane < far, old, gone)
                    old = gone
                sum_ref[index, c] = total
                if emit and c >= HALO:
                    best[c] = total if best[c] is None else jnp.maximum(best[c], total)
        if emit:
            for c in range(HALO, TILES):
                best_ref[c - HALO, pl.ds(t - SEQ + 1, 8, stride=32)] = best[c] * (1.0 / math.sqrt(SEQ))

    def phase(first, last, begin, drop, emit):
        def body(t, carry):
            step(t, begin, drop, emit)
            return carry

        lax.fori_loop(first, last, body, 0, unroll=2)

    phase(0, SEQ - 1, 0, False, False)
    step(SEQ - 1, 0, False, True)
    phase(SEQ, 34, 0, True, True)
    phase(34, 43, 1, True, True)
    phase(43, steps, 2, True, True)
    for c in range(COLUMNS // LANES):
        out_ref[:, tile(c)] = best_ref[c]


SMEM = pl.BlockSpec(memory_space=pltpu.SMEM)
VMEM = pl.BlockSpec(memory_space=pltpu.VMEM)
SPLIT = pltpu.VMEM((6, ROWS, 8 * LANES), jnp.bfloat16)


def local(queries, map_descriptors, slopes):
    ma = lax.axis_index("ma")
    pb = lax.axis_index("pb")
    rows, frames = gather(queries[0], map_descriptors)
    y, x, core = pb // 4, pb // 2 % 2, pb % 2
    at = []
    for dy, dx in ((0, 0),) + SHIFTS:
        chip = (y - dy + 4) % 4 * 2 + (x - dx + 2) % 2
        at += [2 * chip + core, 2 * chip + 1 - core]
    at = jnp.stack([jnp.asarray(v, jnp.int32) for v in at + [ma % 2]])
    block = lambda width: jax.ShapeDtypeStruct((ROWS, width), jnp.float32)
    limit = pltpu.CompilerParams(vmem_limit_bytes=40 << 20)
    rows_scratch = pltpu.VMEM((ROWS, 2048), jnp.bfloat16)
    lines = lambda count: jax.ShapeDtypeStruct((count, LANES), jnp.float32)
    last, lead, left, right = pl.pallas_call(
        edge_kernel,
        name="edges",
        out_shape=(block(LEFT), block(LANES), lines(2 * ROWS + THIRD), lines(THIRD)),
        in_specs=[SMEM] + [VMEM] * 8,
        out_specs=(VMEM,) * 4,
        scratch_shapes=[rows_scratch],
        compiler_params=limit,
        cost_estimate=pl.CostEstimate(flops=2 * ROWS * 512 * 2048, bytes_accessed=6 << 20, transcendentals=0),
    )(at, *rows, *frames)
    left = lax.ppermute(left, "ma", [(i, i + 1) for i in range(31)])
    right = lax.ppermute(right, "ma", [(i + 1, i) for i in range(31)])
    after, inner = pl.pallas_call(
        middle_kernel,
        name="middle",
        out_shape=(block(LANES), jax.ShapeDtypeStruct((LAST - FIRST, ROWS, LANES), jnp.float32)),
        in_specs=[SMEM] + [VMEM] * 10,
        out_specs=(VMEM,) * 2,
        scratch_shapes=[rows_scratch, pltpu.VMEM((ROWS, 512), jnp.float32), SPLIT],
        compiler_params=limit,
        cost_estimate=pl.CostEstimate(flops=8 * ROWS * 512 * 2048, bytes_accessed=16 << 20, transcendentals=0),
    )(at, *rows, *frames, last, lead)
    marks = jnp.concatenate([slopes, ma[None].astype(jnp.int32)])
    best = best_of(marks, left, right, last, lead, after, inner)
    return best[None]


def best_of(marks, left, right, last, lead, after, inner):
    return pl.pallas_call(
        best_kernel,
        name="best",
        out_shape=jax.ShapeDtypeStruct((ROWS - TOP, COLUMNS), jnp.float32),
        in_specs=[SMEM] + [VMEM] * 6,
        out_specs=VMEM,
        scratch_shapes=[
            SPLIT,
            pltpu.VMEM((5, ROWS, LANES), jnp.float32),
            pltpu.VMEM((SEQ + 31, TILES + HALO, 8, LANES), jnp.float32),
            pltpu.VMEM((8, TILES, 8, LANES), jnp.float32),
            pltpu.VMEM((COLUMNS // LANES, ROWS - TOP, LANES), jnp.float32),
        ],
        compiler_params=pltpu.CompilerParams(vmem_limit_bytes=40 << 20),
        cost_estimate=pl.CostEstimate(flops=60 << 20, bytes_accessed=4 << 20, transcendentals=0),
    )(marks, left, right, last, lead, after, inner)


def solution(mesh):
    return jax.shard_map(
        local,
        mesh=mesh,
        in_specs=(P(None, ("pb", "ma"), None), P("ma", "pb"), P()),
        out_specs=P(None, "pb", "ma"),
        check_vma=False,
    )
```

```python
import functools
import math

import jax
import jax.numpy as jnp
from jax import lax
from jax.experimental import pallas as pl
from jax.experimental.pallas import tpu as pltpu
from jax.sharding import PartitionSpec as P

SEQ = 20
RAD = 10
TOP = 32
LEFT = 384
LANES = 128
ROWS = TOP + 256
COLUMNS = 1024
THIRD = ROWS // 3
PACK = 40
HALO = LEFT // LANES
TILES = HALO + COLUMNS // LANES
FIRST, LAST = HALO + 1, TILES - 1
SHIFTS = ((1, 0), (3, 0), (0, 1), (1, 1), (3, 1), (2, 0), (2, 1))


def tile(c):
    return slice(c * LANES, (c + 1) * LANES)


def across(dy, dx, core):
    return [
        (y * 4 + x * 2 + c, (y + dy) % 4 * 4 + (x + dx) % 2 * 2 + (c ^ core))
        for y in range(4)
        for x in range(2)
        for c in range(2)
    ]


def gather(queries, frames):
    depth = queries.shape[-1]
    groups = [[z * 2 + side for z in range(16)] for side in range(2)]
    sides = [(i, i ^ 1) for i in range(32)]
    copies = jnp.broadcast_to(queries[None], (16,) + queries.shape)
    copies, frames = lax.optimization_barrier((copies, frames))
    near = lax.all_to_all(copies, "ma", 0, 0, axis_index_groups=groups)
    own = [frames] + [lax.ppermute(frames, "pb", across(dy, dx, 0)) for dy, dx in SHIFTS]
    own = [jnp.stack(own[:4]), jnp.stack(own[4:])]
    near_top = lax.ppermute(near[14:], "pb", [(i, i + 1) for i in range(15)])
    parts = [lax.ppermute(near[8:], "ma", sides), lax.ppermute(near[:8], "ma", sides)]
    far_top = lax.ppermute(parts[0][6:], "pb", [(i, i + 1) for i in range(15)])
    own[1], parts[0], near_top = lax.optimization_barrier((own[1], parts[0], near_top))
    far = jnp.concatenate(parts[::-1])
    other = [lax.ppermute(part, "pb", across(0, 0, 1)) for part in own]
    rows = [v.reshape(-1, depth) for v in (near, far, near_top, far_top)]
    return rows, own + other


def fill_rows(refs, rows_ref):
    at = 0
    for ref in refs:
        rows_ref[at : at + ref.shape[0]] = ref[...]
        at += ref.shape[0]


def products(at_ref, rows_ref, map_refs, begin, width):
    total = None
    for g in range(8):
        one = pl.multiple_of(at_ref[2 * g] * LANES, LANES)
        two = pl.multiple_of(at_ref[2 * g + 1] * LANES, LANES)
        lhs = jnp.concatenate([rows_ref[:, pl.ds(one, LANES)], rows_ref[:, pl.ds(two, LANES)]], axis=1)
        own, other = map_refs[g // 4], map_refs[2 + g // 4]
        rhs = jnp.concatenate([own[g % 4, pl.ds(begin, width)], other[g % 4, pl.ds(begin, width)]], axis=1)
        part = lax.dot_general(lhs, rhs, (((1,), (1,)), ((), ())), preferred_element_type=jnp.float32)
        total = part if total is None else total + part
    return total


def place_rows(side, out_ref, cols, value):
    for r in range(ROWS // 8):
        if r < 32:
            start, far = TOP + 16 * (r % 16), r // 16
        else:
            start, far = 16 * (r % 2), (r - 32) // 2
        start = pl.multiple_of(start + 8 * (side if far == 0 else 1 - side), 8)
        out_ref[pl.ds(start, 8), cols] = value[8 * r : 8 * r + 8]


def packed(ref, cols, first):
    lane = lax.broadcasted_iota(jnp.int32, (THIRD, LANES), 1)
    parts = [
        pltpu.roll(ref[g * THIRD : (g + 1) * THIRD, cols], (PACK * g - first) % LANES, 1)
        for g in range(3)
    ]
    return jnp.where(lane < PACK, parts[0], jnp.where(lane < 2 * PACK, parts[1], parts[2]))


def unpacked(value, first):
    parts = [pltpu.roll(value, (first - PACK * g) % LANES, 1) for g in range(3)]
    return jnp.concatenate(parts)


def edge_kernel(at_ref, *refs):
    row_refs, map_refs = refs[:4], refs[4:8]
    last_ref, lead_ref, left_ref, rows_ref = refs[8:]
    fill_rows(row_refs, rows_ref)
    side = at_ref[16]
    begin = COLUMNS - LEFT
    for at, width in ((0, 256), (256, 128)):
        value = products(at_ref, rows_ref, map_refs, begin + at, width)
        place_rows(side, last_ref, slice(at, at + width), value)
    place_rows(side, lead_ref, slice(0, LANES), products(at_ref, rows_ref, map_refs, 0, LANES))
    left_ref[:ROWS] = last_ref[:, tile(1)]
    left_ref[ROWS : 2 * ROWS] = last_ref[:, tile(2)]
    left_ref[2 * ROWS :] = packed(last_ref, tile(0), LANES - PACK)


def split_tile(split_ref, slot, value):
    for kind, rest in enumerate((value, value * value)):
        for part in range(3):
            piece = rest.astype(jnp.bfloat16)
            split_ref[3 * kind + part, :, tile(slot)] = piece
            if part < 2:
                rest = rest - piece.astype(jnp.float32)


def band_of():
    at_in = lax.broadcasted_iota(jnp.int32, (4 * LANES, 2 * LANES), 0)
    at_out = lax.broadcasted_iota(jnp.int32, (4 * LANES, 2 * LANES), 1) + LANES
    return jnp.where(jnp.abs(at_in - at_out) <= RAD, 1.0, 0.0).astype(jnp.bfloat16)


def contrast_pair(split_ref, slot, band, tiles):
    found = []
    for kind in range(2):
        total = None
        for part in range(3):
            lhs = split_ref[3 * kind + part, :, slot * LANES : (slot + 4) * LANES]
            term = jnp.dot(lhs, band, preferred_element_type=jnp.float32)
            total = term if total is None else total + term
        found.append(total * (1.0 / (2 * RAD + 1)))
    mean, square = found
    scale = lax.rsqrt(square - mean * mean + 1.0)
    return [(v - mean[:, tile(i)]) * scale[:, tile(i)] for i, v in enumerate(tiles)]


def middle_kernel(at_ref, *refs):
    row_refs, map_refs = refs[:4], refs[4:8]
    last_ref, lead_ref, next_ref, inner_ref, rows_ref, mid_ref, split_ref = refs[8:]
    fill_rows(row_refs, rows_ref)
    side = at_ref[16]
    for at in (0, 256):
        value = products(at_ref, rows_ref, map_refs, LANES + at, 256)
        place_rows(side, mid_ref, slice(at, at + 256), value)
    next_ref[...] = mid_ref[:, tile(0)]

    def score(c):
        if c == HALO:
            return lead_ref[...]
        if c < HALO + 5:
            return mid_ref[:, tile(c - HALO - 1)]
        return last_ref[:, tile(c - HALO - 5)]

    for c in range(HALO, TILES):
        split_tile(split_ref, c - HALO, score(c))
    band = band_of()
    for c in range(FIRST, LAST, 2):
        values = contrast_pair(split_ref, c - HALO - 1, band, [score(c), score(c + 1)])
        for half, value in enumerate(values):
            inner_ref[c - FIRST + half] = value


def best_kernel(slopes_ref, left_ref, right_ref, last_ref, lead_ref, next_ref, inner_ref, out_ref, split_ref, x_ref, lag_ref, sum_ref, best_ref):
    first_map = slopes_ref[8] == 0
    empty = jnp.zeros((ROWS, LANES), jnp.bfloat16)
    band = band_of()
    farthest = unpacked(left_ref[2 * ROWS :], LANES - PACK)
    edge = [farthest, left_ref[:ROWS], left_ref[ROWS : 2 * ROWS], lead_ref[...], next_ref[...]]
    for part in range(6):
        split_ref[part, :, tile(0)] = empty
    for c, value in enumerate(edge):
        split_tile(split_ref, c + 1, value)
    for c in (0, 2):
        values = contrast_pair(split_ref, c, band, edge[c : c + 2])
        for half, value in enumerate(values):
            if c + half < HALO:
                value = jnp.where(first_map, 0.0, value)
            x_ref[c + half] = value
    edge = [last_ref[:, tile(1)], last_ref[:, tile(2)], right_ref[...]]
    for part in range(6):
        split_ref[part, :, tile(3)] = empty
    for c, value in enumerate(edge):
        split_tile(split_ref, c, value)
    x_ref[4] = contrast_pair(split_ref, 0, band, edge[1:2])[0]

    def contrast_at(c, row):
        take = pl.ds(row, 8, stride=32)
        if c < FIRST:
            return x_ref[c, take]
        return inner_ref[c - FIRST, take] if c < LAST else x_ref[4, take]

    steps = SEQ - 1 + 32
    zero = jnp.zeros((8, LANES), jnp.float32)
    for t in range(steps):
        for c in range(HALO):
            lag_ref[t, c] = zero
        for c in range(TILES):
            lag_ref[t, c + HALO] = contrast_at(c, t + TOP - SEQ + 1)
    for index in range(8):
        for c in range(TILES):
            sum_ref[index, c] = zero

    lane = lax.broadcasted_iota(jnp.int32, (8, LANES), 1)

    def step(t, begin, drop, emit):
        best = [None] * TILES
        for index in range(8):
            v = slopes_ref[index]
            by = v
            far = SEQ * v
            whole = far // LANES
            far = far % LANES
            before = zero
            old = None

            def dropped(c):
                return pltpu.roll(lag_ref[t - SEQ, c + HALO - whole], far, 1)

            if drop:
                old = dropped(begin - 1)
            for c in range(begin, TILES):
                moved = pltpu.roll(sum_ref[index, c], by, 1)
                total = jnp.where(lane < by, before, moved) + lag_ref[t, c + HALO]
                before = moved
                if drop:
                    gone = dropped(c)
                    total = total - jnp.where(lane < far, old, gone)
                    old = gone
                sum_ref[index, c] = total
                if emit and c >= HALO:
                    best[c] = total if best[c] is None else jnp.maximum(best[c], total)
        if emit:
            for c in range(HALO, TILES):
                best_ref[c - HALO, pl.ds(t - SEQ + 1, 8, stride=32)] = best[c] * (1.0 / math.sqrt(SEQ))

    def phase(first, last, begin, drop, emit):
        def body(t, carry):
            step(t, begin, drop, emit)
            return carry

        lax.fori_loop(first, last, body, 0, unroll=2)

    phase(0, SEQ - 1, 0, False, False)
    step(SEQ - 1, 0, False, True)
    phase(SEQ, 34, 0, True, True)
    phase(34, 43, 1, True, True)
    phase(43, steps, 2, True, True)
    for c in range(COLUMNS // LANES):
        out_ref[:, tile(c)] = best_ref[c]


SMEM = pl.BlockSpec(memory_space=pltpu.SMEM)
VMEM = pl.BlockSpec(memory_space=pltpu.VMEM)
SPLIT = pltpu.VMEM((6, ROWS, 8 * LANES), jnp.bfloat16)


def local(queries, map_descriptors, slopes):
    ma = lax.axis_index("ma")
    pb = lax.axis_index("pb")
    rows, frames = gather(queries[0], map_descriptors)
    y, x, core = pb // 4, pb // 2 % 2, pb % 2
    at = []
    for dy, dx in ((0, 0),) + SHIFTS:
        chip = (y - dy + 4) % 4 * 2 + (x - dx + 2) % 2
        at += [2 * chip + core, 2 * chip + 1 - core]
    at = jnp.stack([jnp.asarray(v, jnp.int32) for v in at + [ma % 2]])
    block = lambda width: jax.ShapeDtypeStruct((ROWS, width), jnp.float32)
    limit = pltpu.CompilerParams(vmem_limit_bytes=40 << 20)
    rows_scratch = pltpu.VMEM((ROWS, 2048), jnp.bfloat16)
    lines = lambda count: jax.ShapeDtypeStruct((count, LANES), jnp.float32)
    last, lead, left = pl.pallas_call(
        edge_kernel,
        name="edges",
        out_shape=(block(LEFT), block(LANES), lines(2 * ROWS + THIRD)),
        in_specs=[SMEM] + [VMEM] * 8,
        out_specs=(VMEM,) * 3,
        scratch_shapes=[rows_scratch],
        compiler_params=limit,
        cost_estimate=pl.CostEstimate(flops=2 * ROWS * 512 * 2048, bytes_accessed=6 << 20, transcendentals=0),
    )(at, *rows, *frames)
    left = lax.ppermute(left, "ma", [(i, i + 1) for i in range(31)])
    right = lax.ppermute(lead, "ma", [(i + 1, i) for i in range(31)])
    after, inner = pl.pallas_call(
        middle_kernel,
        name="middle",
        out_shape=(block(LANES), jax.ShapeDtypeStruct((LAST - FIRST, ROWS, LANES), jnp.float32)),
        in_specs=[SMEM] + [VMEM] * 10,
        out_specs=(VMEM,) * 2,
        scratch_shapes=[rows_scratch, pltpu.VMEM((ROWS, 512), jnp.float32), SPLIT],
        compiler_params=limit,
        cost_estimate=pl.CostEstimate(flops=8 * ROWS * 512 * 2048, bytes_accessed=16 << 20, transcendentals=0),
    )(at, *rows, *frames, last, lead)
    marks = jnp.concatenate([slopes, ma[None].astype(jnp.int32)])
    best = best_of(marks, left, right, last, lead, after, inner)
    return best[None]


def best_of(marks, left, right, last, lead, after, inner):
    return pl.pallas_call(
        best_kernel,
        name="best",
        out_shape=jax.ShapeDtypeStruct((ROWS - TOP, COLUMNS), jnp.float32),
        in_specs=[SMEM] + [VMEM] * 6,
        out_specs=VMEM,
        scratch_shapes=[
            SPLIT,
            pltpu.VMEM((5, ROWS, LANES), jnp.float32),
            pltpu.VMEM((SEQ + 31, TILES + HALO, 8, LANES), jnp.float32),
            pltpu.VMEM((8, TILES, 8, LANES), jnp.float32),
            pltpu.VMEM((COLUMNS // LANES, ROWS - TOP, LANES), jnp.float32),
        ],
        compiler_params=pltpu.CompilerParams(vmem_limit_bytes=40 << 20),
        cost_estimate=pl.CostEstimate(flops=60 << 20, bytes_accessed=4 << 20, transcendentals=0),
    )(marks, left, right, last, lead, after, inner)


def solution(mesh):
    return jax.shard_map(
        local,
        mesh=mesh,
        in_specs=(P(None, ("pb", "ma"), None), P("ma", "pb"), P()),
        out_specs=P(None, "pb", "ma"),
        check_vma=False,
    )
```
